32 devices in a mesh: group: 1, node: 8 (over y, x, core), local: 4 (over z).
Axes of the slice: x: 2, y: 2, z: 4, core: 2. Of those that a mesh axis runs over, the one named last changes fastest.
Arguments:
- queries: bfloat16 [256, 64, 128], P(('group', 'node', 'local')), may hold values from -5 to 5
- key_cache: bfloat16 [256, 4, 96, 128], P(('group', 'node', 'local')), may hold values from -5 to 5
- value_cache: bfloat16 [256, 4, 96, 128], P(('group', 'node', 'local')), may hold values from -15 to 15
- fresh_token_keys: bfloat16 [256, 4, 128], P(('group', 'node', 'local')), may hold values from -5 to 5
- new_values: bfloat16 [256, 4, 128], P(('group', 'node', 'local')), may hold values from -15 to 15
- lengths: int32 [256], P(('group', 'node', 'local')), may hold values from 2 to 96, as said below
- hidden_rows: bfloat16 [256, 4096], P(('group', 'node', 'local')), may hold values from -100 to 100
- norm_gain: bfloat16 [4096], replicated, may hold values from 0.099609375 to 1.8984375
- expert_ids: int32 [256, 8], P(('group', 'node', 'local')), may hold values from 0 to 15, all different within a row; in each aligned block of 8 rows (0 to 7, 8 to 15, ...) at most 8 rows name the same one
- route_scores: float32 [256, 8], P(('group', 'node', 'local')), may hold values from 0.1 to 10
- gate_weight: bfloat16 [32, 4096, 768], P(('node', 'local')), may hold values from -0.09375 to 0.09375
- up_weight: bfloat16 [32, 4096, 768], P(('node', 'local')), may hold values from -0.09375 to 0.09375
- down_weight: bfloat16 [32, 768, 4096], P(('node', 'local')), may hold values from -0.4375 to 0.4375
Outputs:
- context: bfloat16 [256, 8192], P(('group', 'node', 'local'))
- weighted_expert_total: bfloat16 [256, 4096], P(('group', 'node', 'local'))
The draws below stay inside these ranges and needn't reach their ends.
Inputs may be any that keep to these rules, and one draw needn't show every extreme that they name: `expert_ids`: each row names 8 different experts; among the 8 rows of one device no expert is named more than 8 times, and on some device some expert is named exactly 8 times. `lengths`: some request has all 96 slots filled.
All inputs are finite; a program needn't handle non-finite values.
Results may differ from the reference program's by a relative error of at most 0.0065.
Values may be sent and summed in bfloat16 or wider, within the bound.
No kernel may reach another device: no remote copies, remote signals or barrier semaphores. Data moves between devices by JAX's collectives and lax.ppermute only.
A program may use at most 128 MiB of HBM per device.

```python
import math
import jax
import jax.numpy as jnp
import numpy as np
from jax import lax

D = 4096
FF = 1536
QH = 64
KVH = 4
HD = 128
TOP = 8
REQ_DEV = 8
CTX = 96
HALF = 768
EXPERTS = 16
MOST = 8
REQS = 256
N_NODE = 8
N_LOCAL = 4


def draw_queries(key, part):
    base_key = jax.random.fold_in(key, 11)
    values = jnp.clip(jax.random.normal(base_key, (REQS, QH, HD), jnp.float32), -4.5, 4.5)
    return values.astype(jnp.bfloat16)


def draw_key_cache(key, part):
    base_key = jax.random.fold_in(key, 13)
    values = jnp.clip(jax.random.normal(base_key, (REQS, KVH, CTX, HD), jnp.float32), -4.5, 4.5)
    return values.astype(jnp.bfloat16)


def draw_lengths(key, part):
    first = jax.random.randint(jax.random.fold_in(key, 21), (REQS,), 2, CTX + 1)
    second = jax.random.randint(jax.random.fold_in(key, 22), (REQS,), 2, CTX + 1)
    chosen = jax.random.randint(jax.random.fold_in(key, 23), (), 0, REQS)
    shorter = jnp.minimum(first, second)
    return jnp.where(jnp.arange(REQS, dtype=jnp.int32) == chosen, CTX, shorter).astype(jnp.int32)


def draw_hidden_rows(key, part):
    base_key = jax.random.fold_in(key, 31)
    row_key = jax.random.fold_in(key, 32)
    column_key = jax.random.fold_in(key, 33)
    column_scale = jnp.exp(jax.random.uniform(column_key, (1, D), jnp.float32, math.log(0.3), math.log(3.0)))
    base = jnp.clip(jax.random.normal(base_key, (REQS, D), jnp.float32), -4.0, 4.0)
    row_scale = jnp.exp(jax.random.uniform(row_key, (REQS, 1), jnp.float32, math.log(0.3), math.log(3.0)))
    return (base * row_scale * column_scale).astype(jnp.bfloat16)


def block_levels(rng, dims, cuts, low, top_value):
    def one(dim, shards_of):
        draws = jax.random.uniform(jax.random.fold_in(jax.random.fold_in(rng, 6), dim), (shards_of,), jnp.float32, low / len(cuts), top_value / len(cuts))
        return jnp.repeat(jnp.exp(draws), dims[dim] // shards_of).reshape((-1,) + (1,) * (len(dims) - dim - 1))

    gain = one(*cuts[0])
    for cut in cuts[1:]:
        gain = gain * one(*cut)
    return gain


def routed_block(rng, own, number, rows, amount, top, reach, slope):
    order = jax.random.permutation(rng, amount)
    heavy_load, usual = load_shares(amount, rows * top, reach, slope, True), load_shares(amount, rows * top, reach, slope, False)
    places = jnp.arange(amount)

    def named(tallies, offset_by):
        used = int((tallies > 0).sum())
        fixed = max(1, used // 4)
        passed = fixed + (places - fixed + offset_by * (used - fixed)) % max(1, amount - fixed)
        return jnp.zeros((amount,), jnp.int32).at[order[jnp.where(places < fixed, places, passed)]].set(jnp.asarray(tallies, jnp.int32))

    tallies = jnp.where(number % 4 == 0, named(heavy_load, number // 4), named(usual, number - number // 4 - 1))
    mixed = jax.random.permutation(jax.random.fold_in(own, 3), amount)
    giver, taker = mixed[0:amount // 2 * 2:2], mixed[1:amount // 2 * 2:2]
    margin = jnp.minimum(tallies[giver] - 1, reach - tallies[taker]) // 2
    margin = jnp.where((giver == order[0]) | (taker == order[0]) | (tallies[taker] == 0), 0, jnp.maximum(margin, 0))
    passed = jax.random.randint(jax.random.fold_in(own, 4), (amount // 2,), 0, 1 << 20) % (margin + 1)
    tallies = tallies.at[giver].add(-passed).at[taker].add(passed)
    members = jnp.searchsorted(jnp.cumsum(tallies), jnp.arange(rows * top), side="right").astype(jnp.int32)
    grid = members.reshape(top, rows).T
    grid = grid[jax.random.permutation(jax.random.fold_in(own, 1), rows)]
    offset_by = jax.random.randint(jax.random.fold_in(own, 2), (rows, 1), 0, top)
    return jnp.take_along_axis(grid, (jnp.arange(top)[None, :] + offset_by) % top, axis=1)


def load_shares(count, total, most, slope, full):
    weights = [(1 << 20) // math.isqrt(rank ** slope) + 1 for rank in range(1, count + 1)]
    largest = most if full else min(most, max(-(-total // count), total * weights[0] // sum(weights)))
    least = 1 if total - largest >= count - 1 else 0
    holding, spare = [largest] + [least] * (count - 1), total - largest - least * (count - 1)
    while spare > 0:
        candidates = [i for i in range(1, count) if holding[i] < largest] or [i for i in range(1, count) if holding[i] < most]
        whole, remaining = sum([weights[i] for i in candidates]), spare
        for i in candidates:
            more = min(most - holding[i], max(1, remaining * weights[i] // whole), spare)
            holding[i] = holding[i] + more
            spare = spare - more
    return np.array(holding)


def scatter_about(rng, dims, scale, reach, split=(), kind=jnp.bfloat16):
    loudness = block_levels(rng, dims, split, -0.22, 0.18) if split else 1.0
    drawn = jax.random.normal(rng, dims, jnp.float32) * scale * loudness
    return jnp.minimum(jnp.maximum(drawn, -reach), reach).astype(kind)


def setup_inputs(seed: int = 0, part: int = 0) -> dict:
    streams_of = jax.random.split(jax.random.key(seed), 14)
    own_keys = jax.random.split(jax.random.fold_in(streams_of[13], part), 14)
    queries = draw_queries(jax.random.fold_in(jax.random.fold_in(streams_of[13], part), 71), part)
    key_cache = draw_key_cache(jax.random.fold_in(jax.random.fold_in(streams_of[13], part), 71), part)
    value_cache = scatter_about(own_keys[2], (REQS, KVH, CTX, HD), 3.0, 15.0, ((0, 32),))
    fresh_token_keys = scatter_about(own_keys[3], (REQS, KVH, HD), 1.0, 5.0, ((0, 32),))
    new_values = scatter_about(own_keys[4], (REQS, KVH, HD), 3.0, 15.0, ((0, 32),))
    lengths = draw_lengths(jax.random.fold_in(jax.random.fold_in(streams_of[13], part), 71), part)
    hidden_rows = draw_hidden_rows(jax.random.fold_in(jax.random.fold_in(streams_of[13], part), 71), part)
    norm_gain = jnp.clip(1.0 + 0.18 * jax.random.normal(streams_of[7], (D,), jnp.float32), 0.099609375, 1.8984375).astype(jnp.bfloat16)
    expert_ids_keys = jax.random.split(jax.random.fold_in(own_keys[8], 1), REQS // REQ_DEV)
    expert_ids_turns = jax.random.permutation(jax.random.fold_in(own_keys[8], 3), REQS // REQ_DEV)
    expert_ids = jax.vmap(lambda own, number: routed_block(jax.random.fold_in(own_keys[8], 2), own, number, REQ_DEV, EXPERTS, TOP, MOST, 2))(expert_ids_keys, expert_ids_turns).reshape((REQS, TOP))
    route_scores = jnp.clip(jnp.exp(math.log(10.0) - 4.6051702 * jax.random.uniform(own_keys[9], (REQS, TOP), jnp.float32) ** block_levels(own_keys[9], (REQS, TOP), ((0, 32),), -0.2, 0.2)), 0.1, 10.0)
    gate_weight = scatter_about(streams_of[10], (2 * EXPERTS, D, HALF), D ** -0.5, 0.09375, ((0, 32),))
    up_weight = scatter_about(streams_of[11], (2 * EXPERTS, D, HALF), D ** -0.5, 0.09375, ((0, 32),))
    down_weight = scatter_about(streams_of[12], (2 * EXPERTS, HALF, D), (FF // 8) ** -0.5, 0.4375, ((0, 32),))
    return dict(queries=queries, key_cache=key_cache, value_cache=value_cache, fresh_token_keys=fresh_token_keys, new_values=new_values, lengths=lengths, hidden_rows=hidden_rows, norm_gain=norm_gain, expert_ids=expert_ids, route_scores=route_scores, gate_weight=gate_weight, up_weight=up_weight, down_weight=down_weight)


def attend_block(queries, key_cache, value_cache, fresh_token_keys, new_values, lengths):
    request_count = queries.shape[0]
    grouped_queries = queries.astype(jnp.float32).reshape(request_count, KVH, QH // KVH, HD)
    keys_f32 = key_cache.astype(jnp.float32)
    values_f32 = value_cache.astype(jnp.float32)
    inverse_scale = 1.0 / math.sqrt(HD)
    scores = jnp.einsum('bkgd,bkpd->bkgp', grouped_queries, keys_f32, precision=lax.Precision.HIGHEST) * inverse_scale
    positions = jnp.arange(CTX, dtype=jnp.int32)
    in_range = positions[None, :] < lengths[:, None]
    scores = jnp.where(in_range[:, None, None, :], scores, -jnp.inf)
    self_token_score = jnp.einsum('uxea,uxa->uxe', grouped_queries, fresh_token_keys.astype(jnp.float32), precision=lax.Precision.HIGHEST) * inverse_scale
    highest = jnp.maximum(lax.optimization_barrier(jnp.max(scores, axis=-1)), self_token_score)
    exponent = jnp.exp(scores - highest[..., None])
    own_exponent = jnp.exp(self_token_score - highest)
    denominator = lax.optimization_barrier(jnp.sum(exponent, axis=-1)) + own_exponent
    probs = lax.optimization_barrier((exponent / denominator[..., None]).astype(jnp.bfloat16)).astype(jnp.float32)
    own_prob = lax.optimization_barrier((own_exponent / denominator).astype(jnp.bfloat16)).astype(jnp.float32)
    mixed = jnp.einsum('bkgp,bkpd->bkgd', probs, values_f32, precision=lax.Precision.HIGHEST)
    mixed = mixed + own_prob[..., None] * new_values.astype(jnp.float32)[:, :, None, :]
    return mixed.reshape(request_count, QH * HD).astype(jnp.bfloat16)

def reference(queries, key_cache, value_cache, fresh_token_keys, new_values, lengths, hidden_rows, norm_gain, expert_ids, route_scores, gate_weight, up_weight, down_weight):
    blocks = REQS // REQ_DEV
    packed = (queries.reshape(blocks, REQ_DEV, QH, HD), key_cache.reshape(blocks, REQ_DEV, KVH, CTX, HD), value_cache.reshape(blocks, REQ_DEV, KVH, CTX, HD), fresh_token_keys.reshape(blocks, REQ_DEV, KVH, HD), new_values.reshape(blocks, REQ_DEV, KVH, HD), lengths.reshape(blocks, REQ_DEV))
    context = lax.map(lambda pieces: attend_block(*pieces), packed).reshape(REQS, QH * HD)
    hidden_f32 = hidden_rows.astype(jnp.float32)
    mean_square = lax.optimization_barrier(jnp.mean(hidden_f32 * hidden_f32, axis=1, keepdims=True))
    normed = (hidden_f32 * lax.rsqrt(mean_square + 1e-06) * norm_gain.astype(jnp.float32)).astype(jnp.bfloat16)
    gates = route_scores / lax.optimization_barrier(jnp.sum(route_scores, axis=1, keepdims=True))
    capacity_all = N_NODE * N_LOCAL * MOST

    def one_expert(total, expert_index):
        chosen = expert_ids == expert_index
        weighting = lax.optimization_barrier(jnp.sum(jnp.where(chosen, gates, 0.0), axis=1))
        reached_mask = jnp.any(chosen, axis=1)
        picked = jnp.nonzero(reached_mask, size=capacity_all, fill_value=0)[0].astype(jnp.int32)
        reached_count = jnp.sum(reached_mask.astype(jnp.int32))
        live = jnp.arange(capacity_all, dtype=jnp.int32) < reached_count
        gate_pair = lax.dynamic_slice_in_dim(gate_weight, 2 * expert_index, 2, 0)
        up_pair = lax.dynamic_slice_in_dim(up_weight, 2 * expert_index, 2, 0)
        down_pair = lax.dynamic_slice_in_dim(down_weight, 2 * expert_index, 2, 0)
        gate_full = jnp.concatenate([gate_pair[0], gate_pair[1]], axis=1)
        up_full = jnp.concatenate([up_pair[0], up_pair[1]], axis=1)
        down_full = down_pair.reshape(2 * HALF, D)
        selected = normed[picked]
        gate_proj = jnp.dot(selected, gate_full, preferred_element_type=jnp.float32)
        up_proj = jnp.dot(selected, up_full, preferred_element_type=jnp.float32)
        activated = (jax.nn.silu(gate_proj) * up_proj).astype(jnp.bfloat16)
        produced = jnp.dot(activated, down_full, preferred_element_type=jnp.float32)
        scaled = jnp.where(live[:, None], weighting[picked][:, None] * produced, 0.0)
        return (total.at[picked].add(scaled), None)
    total, unused = lax.scan(one_expert, jnp.zeros((REQS, D), jnp.float32), jnp.arange(EXPERTS, dtype=jnp.int32))
    return (context, total.astype(jnp.bfloat16))
```

```python
import math

import jax
import jax.numpy as jnp
from jax import lax
from jax.sharding import PartitionSpec as P


def attend(queries, key_cache, value_cache, fresh_token_keys, new_values, lengths):
    request_count, head_count, head_width = queries.shape
    kv_heads = key_cache.shape[1]
    slot_count = key_cache.shape[2]
    grouped_queries = queries.reshape(request_count, kv_heads, head_count // kv_heads, head_width)
    inverse_scale = 1.0 / math.sqrt(head_width)
    scores = (
        jnp.einsum(
            "bkgd,bkpd->bkgp", grouped_queries, key_cache, preferred_element_type=jnp.float32
        )
        * inverse_scale
    )
    positions = jnp.arange(slot_count, dtype=jnp.int32)
    in_range = positions[None, :] < lengths[:, None]
    scores = jnp.where(in_range[:, None, None, :], scores, -jnp.inf)
    self_token_score = (
        jnp.einsum(
            "uxea,uxa->uxe", grouped_queries, fresh_token_keys, preferred_element_type=jnp.float32
        )
        * inverse_scale
    )
    highest = jnp.maximum(jnp.max(scores, axis=-1), self_token_score)
    exponent = jnp.exp(scores - highest[..., None])
    own_exponent = jnp.exp(self_token_score - highest)
    denominator = jnp.sum(exponent, axis=-1) + own_exponent
    probs = (exponent / denominator[..., None]).astype(jnp.bfloat16)
    own_prob = (own_exponent / denominator).astype(jnp.bfloat16)
    mixed = jnp.einsum("bkgp,bkpd->bkgd", probs, value_cache, preferred_element_type=jnp.float32)
    mixed = (
        mixed
        + own_prob.astype(jnp.float32)[..., None] * new_values.astype(jnp.float32)[:, :, None, :]
    )
    return mixed.reshape(request_count, head_count * head_width).astype(jnp.bfloat16)


def exchange(rows, node_mask, local_mask):
    nodes = lax.axis_size("node")
    locals_ = lax.axis_size("local")
    pairs = [
        (n * locals_ + k, (n ^ node_mask) * locals_ + (k ^ local_mask))
        for n in range(nodes)
        for k in range(locals_)
    ]
    return lax.ppermute(rows, ("node", "local"), pairs)


def gather_rows(rows):
    nodes = lax.axis_size("node")
    line = jnp.concatenate(
        [rows] + [exchange(rows, 0, k) for k in range(1, lax.axis_size("local"))]
    )
    plane = jnp.concatenate([line] + [exchange(line, n, 0) for n in range(2, nodes, 2)])
    return jnp.concatenate([plane, exchange(plane, 1, 0)])


def scatter_sum(partial_rows):
    nodes = lax.axis_size("node")
    locals_ = lax.axis_size("local")
    half = partial_rows.shape[0] // 2
    arrived = exchange(partial_rows[half:].astype(jnp.bfloat16), 1, 0)
    plane = partial_rows[:half] + arrived.astype(jnp.float32)
    size = half // (nodes // 2)
    packed = plane.astype(jnp.bfloat16)
    line = plane[:size]
    for step in range(1, nodes // 2):
        line = line + exchange(
            packed[step * size : (step + 1) * size], 2 * step, 0
        ).astype(jnp.float32)
    size = size // locals_
    packed = line.astype(jnp.bfloat16)
    total = line[:size]
    for step in range(1, locals_):
        total = total + exchange(
            packed[step * size : (step + 1) * size], 0, step
        ).astype(jnp.float32)
    return total


def per_device(
    queries,
    key_cache,
    value_cache,
    fresh_token_keys,
    new_values,
    lengths,
    hidden_rows,
    norm_gain,
    expert_ids,
    route_scores,
    gate_weight,
    up_weight,
    down_weight,
):
    context = attend(queries, key_cache, value_cache, fresh_token_keys, new_values, lengths)
    row_count, model_width = hidden_rows.shape
    experts = lax.axis_size("node") * lax.axis_size("local") // 2
    hidden_f32 = hidden_rows.astype(jnp.float32)
    mean_square = jnp.mean(hidden_f32 * hidden_f32, axis=1, keepdims=True)
    normed = (hidden_f32 * lax.rsqrt(mean_square + 1e-06) * norm_gain.astype(jnp.float32)).astype(
        jnp.bfloat16
    )
    gates = route_scores / jnp.sum(route_scores, axis=1, keepdims=True)
    chosen = expert_ids[:, :, None] == jnp.arange(experts, dtype=jnp.int32)[None, None, :]
    table = jnp.sum(jnp.where(chosen, gates[:, :, None], 0.0), axis=1)
    coarse = lax.reduce_precision(table, 8, 7)
    extra = -(2 * experts) % 128
    outgoing = jnp.concatenate(
        [
            normed,
            coarse.astype(jnp.bfloat16),
            (table - coarse).astype(jnp.bfloat16),
            jnp.zeros((row_count, extra), jnp.bfloat16),
        ],
        axis=1,
    )
    arrived = gather_rows(outgoing)
    tokens = arrived[:, :model_width]
    own = (lax.axis_index("node") * lax.axis_size("local") + lax.axis_index("local")) // 2
    column = jnp.arange(2 * experts + extra, dtype=jnp.int32) % experts
    mine = (column == own) & (jnp.arange(2 * experts + extra) < 2 * experts)
    weight = jnp.sum(
        jnp.where(mine[None, :], arrived[:, model_width:].astype(jnp.float32), 0.0),
        axis=1,
        keepdims=True,
    )
    gate_proj = jnp.dot(tokens, gate_weight[0], preferred_element_type=jnp.float32)
    up_proj = jnp.dot(tokens, up_weight[0], preferred_element_type=jnp.float32)
    activated = (jax.nn.silu(gate_proj) * up_proj).astype(jnp.bfloat16)
    partial_rows = weight * jnp.dot(activated, down_weight[0], preferred_element_type=jnp.float32)
    return (context, scatter_sum(partial_rows).astype(jnp.bfloat16))


def solution(mesh):
    placed = (
        P(("group", "node", "local"), None, None),
        P(("group", "node", "local"), None, None, None),
        P(("group", "node", "local"), None, None, None),
        P(("group", "node", "local"), None, None),
        P(("group", "node", "local"), None, None),
        P(("group", "node", "local")),
        P(("group", "node", "local"), None),
        P(),
        P(("group", "node", "local"), None),
        P(("group", "node", "local"), None),
        P(("node", "local"), None, None),
        P(("node", "local"), None, None),
        P(("node", "local"), None, None),
    )
    return jax.shard_map(
        per_device,
        mesh=mesh,
        in_specs=placed,
        out_specs=(P(("group", "node", "local"), None), P(("group", "node", "local"), None)),
        check_vma=False,
    )
```

```python
import functools
import math

import jax
import jax.numpy as jnp
from jax import lax
from jax.experimental import pallas as pl
from jax.experimental.pallas import tpu as pltpu
from jax.sharding import PartitionSpec as P


def attend(queries, key_cache, value_cache, fresh_token_keys, new_values, lengths):
    request_count, head_count, head_width = queries.shape
    kv_heads = key_cache.shape[1]
    slot_count = key_cache.shape[2]
    grouped_queries = queries.reshape(request_count, kv_heads, head_count // kv_heads, head_width)
    inverse_scale = 1.0 / math.sqrt(head_width)
    scores = (
        jnp.einsum(
            "bkgd,bkpd->bkgp", grouped_queries, key_cache, preferred_element_type=jnp.float32
        )
        * inverse_scale
    )
    positions = jnp.arange(slot_count, dtype=jnp.int32)
    in_range = positions[None, :] < lengths[:, None]
    scores = jnp.where(in_range[:, None, None, :], scores, -jnp.inf)
    self_token_score = (
        jnp.einsum(
            "uxea,uxa->uxe", grouped_queries, fresh_token_keys, preferred_element_type=jnp.float32
        )
        * inverse_scale
    )
    highest = jnp.maximum(jnp.max(scores, axis=-1), self_token_score)
    exponent = jnp.exp(scores - highest[..., None])
    own_exponent = jnp.exp(self_token_score - highest)
    denominator = jnp.sum(exponent, axis=-1) + own_exponent
    probs = (exponent / denominator[..., None]).astype(jnp.bfloat16)
    own_prob = (own_exponent / denominator).astype(jnp.bfloat16)
    mixed = jnp.einsum("bkgp,bkpd->bkgd", probs, value_cache, preferred_element_type=jnp.float32)
    mixed = (
        mixed
        + own_prob.astype(jnp.float32)[..., None] * new_values.astype(jnp.float32)[:, :, None, :]
    )
    return mixed.reshape(request_count, head_count * head_width).astype(jnp.bfloat16)


MIB = 1024 * 1024
TILE = 256
DOWN_TILE = 1024
LOAD_LIMIT = 34 * MIB


def whole(space):
    return pl.BlockSpec(memory_space=space)


def prepare_kernel(
    experts, hidden_hbm, gain_hbm, ids_hbm, scores_hbm, out_ref, hidden_ref, gain_ref, ids_ref, scores_ref, sems
):
    pairs = ((hidden_hbm, hidden_ref), (gain_hbm, gain_ref), (ids_hbm, ids_ref), (scores_hbm, scores_ref))
    copies = [pltpu.make_async_copy(a, b, sems.at[n]) for n, (a, b) in enumerate(pairs)]
    for copy in copies:
        copy.start()
    for copy in copies:
        copy.wait()
    width = hidden_ref.shape[1]
    hidden = hidden_ref[...].astype(jnp.float32)
    mean_square = jnp.mean(hidden * hidden, axis=1, keepdims=True)
    gain = gain_ref[...].astype(jnp.float32).reshape(1, width)
    out_ref[:, :width] = (hidden * lax.rsqrt(mean_square + 1e-06) * gain).astype(jnp.bfloat16)
    scores = scores_ref[...]
    gates = scores / jnp.sum(scores, axis=1, keepdims=True)
    ids = ids_ref[...]
    rows, extra = out_ref.shape[0], out_ref.shape[1] - width
    column = lax.broadcasted_iota(jnp.int32, (rows, extra), 1)
    expert = jnp.where(column < experts, column, column - experts)
    table = jnp.zeros((rows, extra), jnp.float32)
    for j in range(ids.shape[1]):
        table = table + jnp.where(ids[:, j : j + 1] == expert, gates[:, j : j + 1], 0.0)
    coarse = table.astype(jnp.bfloat16).astype(jnp.float32)
    parts = jnp.where(column < experts, coarse, jnp.where(column < 2 * experts, table - coarse, 0.0))
    out_ref[:, width:] = parts.astype(jnp.bfloat16)


def prepare(hidden_rows, norm_gain, expert_ids, route_scores, experts):
    rows, width = hidden_rows.shape
    extra = -(-2 * experts // 128) * 128
    args = (hidden_rows, norm_gain, expert_ids, route_scores)
    return pl.pallas_call(
        functools.partial(prepare_kernel, experts),
        out_shape=pltpu.VMEM((rows, width + extra), jnp.bfloat16),
        in_specs=[whole(pltpu.HBM)] * 4,
        out_specs=whole(pltpu.VMEM),
        scratch_shapes=[pltpu.VMEM(a.shape, a.dtype) for a in args] + [pltpu.SemaphoreType.DMA((4,))],
        compiler_params=pltpu.CompilerParams(vmem_limit_bytes=56 * MIB),
        name="prepare",
    )(*args)


def pack_kernel(tail, after, *refs):
    refs = refs[after:]
    out_ref, tail_ref = refs[-2:] if tail else (refs[-1], None)
    refs = refs[: -2 if tail else -1]
    start, inner = 0, 0
    for n, ref in enumerate(refs):
        out_ref[start : start + ref.shape[0], :] = ref[...]
        start += ref.shape[0]
        if n >= len(refs) - tail:
            tail_ref[inner : inner + ref.shape[0], :] = ref[...]
            inner += ref.shape[0]


def pack(pieces, tail=0, after=()):
    width, dtype = pieces[0].shape[1], pieces[0].dtype

    def out(pieces):
        return pltpu.VMEM((sum(piece.shape[0] for piece in pieces), width), dtype)

    vmem = whole(pltpu.VMEM)
    return pl.pallas_call(
        functools.partial(pack_kernel, tail, len(after)),
        out_shape=(out(pieces), out(pieces[-tail:])) if tail else out(pieces),
        in_specs=[whole(pl.ANY)] * len(after) + [vmem] * len(pieces),
        out_specs=(vmem, vmem) if tail else vmem,
        compiler_params=pltpu.CompilerParams(vmem_limit_bytes=MIB),
        name="pack",
    )(*after, *pieces)


def experts_kernel(experts, load, *refs):
    if load:
        own_ref, here_ref, there_ref = refs[:3]
        sources, (out_here, out_there), held, scratch = refs[3:6], refs[6:8], refs[8:11], refs[11:]
        rows_v, act_v, sems = scratch
    else:
        own_ref, here_ref, there_ref = refs[:3]
        held, (out_here, out_there), (rows_v, act_v) = refs[3:6], refs[6:8], refs[8:]
    gate_ref, up_ref, down_ref = held
    hidden, width = down_ref.shape
    cuts = [pl.ds(t, TILE) for t in range(0, hidden, TILE)]
    down_cuts = [pl.ds(t, DOWN_TILE) for t in range(0, width, DOWN_TILE)]
    copies, waits = [], iter(())
    if load:
        order = [(n, cut) for cut in cuts for n in (0, 1)] + [(2, cut) for cut in down_cuts]
        for k, (n, cut) in enumerate(order):
            copies.append(
                pltpu.make_async_copy(sources[n].at[0, :, cut], held[n].at[:, cut], sems.at[k])
            )
        for copy in copies:
            copy.start()
        waits = iter(copies)

    def arrive(count):
        for _ in range(count if load else 0):
            next(waits).wait()

    half = here_ref.shape[0]
    rows_v[:half, :] = here_ref[:, :width]
    rows_v[half:, :] = there_ref[:, :width]
    column = lax.broadcasted_iota(jnp.int32, (1, here_ref.shape[1] - width), 1)
    mine = (column == own_ref[0]) | (column == own_ref[0] + experts)

    def weights_of(ref):
        parts = jnp.where(mine, ref[:, width:].astype(jnp.float32), 0.0)
        return jnp.sum(parts, axis=1, keepdims=True)

    weight_here, weight_there = weights_of(here_ref), weights_of(there_ref)
    for cut in cuts:
        arrive(2)
        gate = jnp.dot(rows_v[...], gate_ref[:, cut], preferred_element_type=jnp.float32)
        up = jnp.dot(rows_v[...], up_ref[:, cut], preferred_element_type=jnp.float32)
        act_v[:, cut] = (gate / (1.0 + jnp.exp(-gate)) * up).astype(jnp.bfloat16)
    for cut in down_cuts:
        arrive(1)
        produced = jnp.dot(act_v[...], down_ref[:, cut], preferred_element_type=jnp.float32)
        out_here[:, cut] = (weight_here * produced[:half]).astype(jnp.bfloat16)
        out_there[:, cut] = (weight_there * produced[half:]).astype(jnp.bfloat16)


def expert_piece(here, there, own, experts, pieces, load):
    half = here.shape[0]
    hidden, width = pieces[2].shape[-2:]
    out = pltpu.VMEM((half, width), jnp.bfloat16)
    vmem = whole(pltpu.VMEM)
    held = [pltpu.VMEM(piece.shape[1:], piece.dtype) for piece in pieces] if load else []
    scratch = [
        pltpu.VMEM((2 * half, width), jnp.bfloat16),
        pltpu.VMEM((2 * half, hidden), jnp.bfloat16),
    ]
    if load:
        scratch.append(pltpu.SemaphoreType.DMA((2 * (hidden // TILE) + width // DOWN_TILE,)))
    limit = LOAD_LIMIT if load else 64 * half * 1024 + 4 * MIB
    return pl.pallas_call(
        functools.partial(experts_kernel, experts, load),
        out_shape=(out, out, *held),
        in_specs=[whole(pltpu.SMEM), vmem, vmem] + [whole(pltpu.HBM) if load else vmem] * 3,
        out_specs=(vmem,) * (2 + len(held)),
        scratch_shapes=scratch,
        compiler_params=pltpu.CompilerParams(vmem_limit_bytes=limit),
        cost_estimate=pl.CostEstimate(
            flops=12 * half * width * hidden,
            bytes_accessed=6 * width * hidden if load else 0,
            transcendentals=2 * half * hidden,
        ),
        name="expert_piece",
    )(own.reshape(1), here, there, *pieces)


def exchange(rows, node_mask, local_mask):
    nodes = lax.axis_size("node")
    locals_ = lax.axis_size("local")
    pairs = [
        (n * locals_ + k, (n ^ node_mask) * locals_ + (k ^ local_mask))
        for n in range(nodes)
        for k in range(locals_)
    ]
    return lax.ppermute(rows, ("node", "local"), pairs)


def masks():
    far = list(range(2, lax.axis_size("local"))) + [1]
    return far, [lax.axis_size("node") - 2] + list(range(2, lax.axis_size("node") - 2, 2))


def gather_first(rows):
    far, plane = masks()
    line = [exchange(rows, 0, k) for k in far]
    beside = [exchange(rows, n, 0) for n in plane]
    return pack([rows] + beside + line, tail=len(far))


def gather_second(line, after):
    return pack([exchange(line, n, 0) for n in masks()[1]], after=(after,))


def scatter_sum(first, first_other, second, second_other, count):
    far, plane = masks()
    lines = len(far) * count
    cut = first.shape[0] - lines

    def f32(x):
        return x.astype(jnp.float32)

    def block(x, size, i):
        return x[i * size : (i + 1) * size]

    sums = f32(first) + f32(exchange(first_other, 1, 0))
    beside = sums[count:cut].astype(jnp.bfloat16)
    own, line = sums[:count], sums[cut:]
    for i, n in enumerate(plane):
        own = own + f32(exchange(block(beside, count, i), n, 0))
    sums = (f32(second) + f32(exchange(second_other, 1, 0))).astype(jnp.bfloat16)
    sums, own = lax.optimization_barrier((sums, own))
    for i, n in enumerate(plane):
        line = line + f32(exchange(block(sums, lines, i), n, 0))
    line = line.astype(jnp.bfloat16)
    for i, k in enumerate(far):
        own = own + f32(exchange(block(line, count, i), 0, k))
    return own.astype(jnp.bfloat16)


def per_device(
    queries,
    key_cache,
    value_cache,
    fresh_token_keys,
    new_values,
    lengths,
    hidden_rows,
    norm_gain,
    expert_ids,
    route_scores,
    gate_weight,
    up_weight,
    down_weight,
):
    context = attend(queries, key_cache, value_cache, fresh_token_keys, new_values, lengths)
    experts = lax.axis_size("node") * lax.axis_size("local") // 2
    own = (lax.axis_index("node") * lax.axis_size("local") + lax.axis_index("local")) // 2
    outgoing = prepare(hidden_rows, norm_gain, expert_ids, route_scores, experts)
    pieces = (gate_weight, up_weight, down_weight)
    first, line = gather_first(outgoing)
    first, first_other, *pieces = expert_piece(first, exchange(first, 1, 0), own, experts, pieces, True)
    second, first_other = lax.optimization_barrier((gather_second(line, first), first_other))
    second, second_other = expert_piece(
        second, exchange(second, 1, 0), own, experts, pieces, False
    )
    total = scatter_sum(first, first_other, second, second_other, hidden_rows.shape[0])
    return (context, total)


def solution(mesh):
    placed = (
        P(("group", "node", "local"), None, None),
        P(("group", "node", "local"), None, None, None),
        P(("group", "node", "local"), None, None, None),
        P(("group", "node", "local"), None, None),
        P(("group", "node", "local"), None, None),
        P(("group", "node", "local")),
        P(("group", "node", "local"), None),
        P(),
        P(("group", "node", "local"), None),
        P(("group", "node", "local"), None),
        P(("node", "local"), None, None),
        P(("node", "local"), None, None),
        P(("node", "local"), None, None),
    )
    return jax.shard_map(
        per_device,
        mesh=mesh,
        in_specs=placed,
        out_specs=(P(("group", "node", "local"), None), P(("group", "node", "local"), None)),
        check_vma=False,
    )
```

```python
import functools
import math

import jax
import jax.numpy as jnp
from jax import lax
from jax.experimental import pallas as pl
from jax.experimental.pallas import tpu as pltpu
from jax.sharding import PartitionSpec as P


MIB = 1024 * 1024
TILE = 256
DOWN_TILE = 1024
ATTEND_LIMIT = 12 * MIB


def whole(space):
    return pl.BlockSpec(memory_space=space)


def in_hbm(array):
    return pltpu.with_memory_space_constraint(array, pltpu.HBM)


def prepare_kernel(
    experts, hidden_hbm, gain_hbm, ids_hbm, scores_hbm, out_ref, hidden_ref, gain_ref, ids_ref, scores_ref, sems
):
    pairs = ((hidden_hbm, hidden_ref), (gain_hbm, gain_ref), (ids_hbm, ids_ref), (scores_hbm, scores_ref))
    copies = [pltpu.make_async_copy(a, b, sems.at[n]) for n, (a, b) in enumerate(pairs)]
    for copy in copies:
        copy.start()
    for copy in copies:
        copy.wait()
    width = hidden_ref.shape[1]
    hidden = hidden_ref[...].astype(jnp.float32)
    mean_square = jnp.mean(hidden * hidden, axis=1, keepdims=True)
    gain = gain_ref[...].astype(jnp.float32).reshape(1, width)
    out_ref[:, :width] = (hidden * lax.rsqrt(mean_square + 1e-06) * gain).astype(jnp.bfloat16)
    scores = scores_ref[...]
    gates = scores / jnp.sum(scores, axis=1, keepdims=True)
    ids = ids_ref[...]
    rows, extra = out_ref.shape[0], out_ref.shape[1] - width
    column = lax.broadcasted_iota(jnp.int32, (rows, extra), 1)
    expert = jnp.where(column < experts, column, column - experts)
    table = jnp.zeros((rows, extra), jnp.float32)
    for j in range(ids.shape[1]):
        table = table + jnp.where(ids[:, j : j + 1] == expert, gates[:, j : j + 1], 0.0)
    coarse = table.astype(jnp.bfloat16).astype(jnp.float32)
    parts = jnp.where(column < experts, coarse, jnp.where(column < 2 * experts, table - coarse, 0.0))
    out_ref[:, width:] = parts.astype(jnp.bfloat16)


def prepare(hidden_rows, norm_gain, expert_ids, route_scores, experts):
    rows, width = hidden_rows.shape
    extra = -(-2 * experts // 128) * 128
    args = (hidden_rows, norm_gain, expert_ids, route_scores)
    return pl.pallas_call(
        functools.partial(prepare_kernel, experts),
        out_shape=pltpu.VMEM((rows, width + extra), jnp.bfloat16),
        in_specs=[whole(pltpu.HBM)] * 4,
        out_specs=whole(pltpu.VMEM),
        scratch_shapes=[pltpu.VMEM(a.shape, a.dtype) for a in args] + [pltpu.SemaphoreType.DMA((4,))],
        compiler_params=pltpu.CompilerParams(vmem_limit_bytes=2 * MIB),
        name="prepare",
    )(*[in_hbm(a) for a in args])


def attend_kernel(
    kv_heads,
    inverse_scale,
    lengths_hbm,
    queries_hbm,
    keys_hbm,
    values_hbm,
    fresh_hbm,
    new_hbm,
    out_ref,
    lengths_ref,
    queries_v,
    keys_v,
    values_v,
    fresh_v,
    new_v,
    mixed_v,
    sems,
):
    requests, slots, width = keys_hbm.shape
    context = slots // kv_heads
    heads = queries_hbm.shape[1]
    group = heads // kv_heads
    pairs = [
        (queries_hbm, queries_v),
        (keys_hbm, keys_v.at[:, pl.ds(0, slots), :]),
        (values_hbm, values_v.at[:, pl.ds(0, slots), :]),
        (fresh_hbm, fresh_v),
        (new_hbm, new_v),
        (lengths_hbm, lengths_ref),
    ]
    copies = [pltpu.make_async_copy(a, b, sems.at[n]) for n, (a, b) in enumerate(pairs)]
    for copy in copies:
        copy.start()
    total = keys_v.shape[1]
    row_group = lax.broadcasted_iota(jnp.int32, (heads, total), 0) // group
    slot = lax.broadcasted_iota(jnp.int32, (heads, total), 1)
    offset = slot - row_group * context
    is_new = slot == slots + row_group
    empty = jnp.zeros((total - slots - kv_heads, width), jnp.float32)
    for copy in copies:
        copy.wait()
    for b in range(requests):
        for cache, token in ((keys_v, fresh_v), (values_v, new_v)):
            tail = jnp.concatenate([token[b].astype(jnp.float32), empty])
            cache[b, slots:, :] = tail.astype(jnp.bfloat16)
    scores = [
        lax.dot_general(
            queries_v[b], keys_v[b], (((1,), (1,)), ((), ())), preferred_element_type=jnp.float32
        )
        for b in range(requests)
    ]
    probs = []
    for b in range(requests):
        valid = (offset >= 0) & (offset < lengths_ref[b]) & (slot < slots) | is_new
        score = jnp.where(valid, scores[b] * inverse_scale, -1e30)
        exponent = jnp.exp(score - jnp.max(score, axis=1, keepdims=True))
        probs.append((exponent / jnp.sum(exponent, axis=1, keepdims=True)).astype(jnp.bfloat16))
    for b in range(requests):
        mixed_v[b * heads : (b + 1) * heads, :] = jnp.dot(
            probs[b], values_v[b], preferred_element_type=jnp.float32
        )
    for h in range(heads):
        rows = mixed_v[pl.ds(h, requests, stride=heads), :]
        out_ref[:, h * width : (h + 1) * width] = rows.astype(jnp.bfloat16)


def attend(queries, key_cache, value_cache, fresh_token_keys, new_values, lengths):
    requests, heads, width = queries.shape
    kv_heads, context = key_cache.shape[1:3]
    slots = kv_heads * context
    total = -(-(slots + kv_heads) // 128) * 128
    cache = pltpu.VMEM((requests, total, width), jnp.bfloat16)
    token = pltpu.VMEM(fresh_token_keys.shape, jnp.bfloat16)
    vmem = whole(pltpu.VMEM)
    return pl.pallas_call(
        functools.partial(attend_kernel, kv_heads, 1.0 / math.sqrt(width)),
        out_shape=jax.ShapeDtypeStruct((requests, heads * width), jnp.bfloat16),
        in_specs=[whole(pltpu.HBM)] * 6,
        out_specs=vmem,
        scratch_shapes=[
            pltpu.SMEM(lengths.shape, jnp.int32),
            pltpu.VMEM(queries.shape, jnp.bfloat16),
            cache,
            cache,
            token,
            token,
            pltpu.VMEM((requests * heads, width), jnp.float32),
            pltpu.SemaphoreType.DMA((6,)),
        ],
        compiler_params=pltpu.CompilerParams(vmem_limit_bytes=ATTEND_LIMIT),
        cost_estimate=pl.CostEstimate(
            flops=12 * 10**9,
            bytes_accessed=4 * key_cache.size,
            transcendentals=requests * heads * total,
        ),
        name="attend",
    )(
        in_hbm(lengths),
        in_hbm(queries),
        in_hbm(key_cache.reshape(requests, slots, width)),
        in_hbm(value_cache.reshape(requests, slots, width)),
        in_hbm(fresh_token_keys),
        in_hbm(new_values),
    )


def pack_kernel(tail, after, *refs):
    refs = refs[after:]
    out_ref, tail_ref = refs[-2:] if tail else (refs[-1], None)
    refs = refs[: -2 if tail else -1]
    start, inner = 0, 0
    for n, ref in enumerate(refs):
        out_ref[start : start + ref.shape[0], :] = ref[...]
        start += ref.shape[0]
        if n >= len(refs) - tail:
            tail_ref[inner : inner + ref.shape[0], :] = ref[...]
            inner += ref.shape[0]


def pack(pieces, tail=0, after=()):
    width, dtype = pieces[0].shape[1], pieces[0].dtype

    def out(pieces):
        return pltpu.VMEM((sum(piece.shape[0] for piece in pieces), width), dtype)

    vmem = whole(pltpu.VMEM)
    return pl.pallas_call(
        functools.partial(pack_kernel, tail, len(after)),
        out_shape=(out(pieces), out(pieces[-tail:])) if tail else out(pieces),
        in_specs=[whole(pl.ANY)] * len(after) + [vmem] * len(pieces),
        out_specs=(vmem, vmem) if tail else vmem,
        compiler_params=pltpu.CompilerParams(vmem_limit_bytes=MIB),
        name="pack",
    )(*after, *pieces)


def experts_kernel(
    experts, after, here_ref, there_ref, gate_ref, up_ref, down_ref, *refs
):
    out_here, out_there, rows_v, act_v = refs[after:]
    hidden, width = down_ref.shape
    cuts = [pl.ds(t, TILE) for t in range(0, hidden, TILE)]
    down_cuts = [pl.ds(t, DOWN_TILE) for t in range(0, width, DOWN_TILE)]
    half = here_ref.shape[0]
    rows_v[:half, :] = here_ref[:, :width]
    rows_v[half:, :] = there_ref[:, :width]
    column = lax.broadcasted_iota(jnp.int32, (1, here_ref.shape[1] - width), 1)
    own = (lax.axis_index("node") * lax.axis_size("local") + lax.axis_index("local")) // 2
    mine = (column == own) | (column == own + experts)

    def weights_of(ref):
        parts = jnp.where(mine, ref[:, width:].astype(jnp.float32), 0.0)
        return jnp.sum(parts, axis=1, keepdims=True)

    weight_here, weight_there = weights_of(here_ref), weights_of(there_ref)
    for cut in cuts:
        gate = jnp.dot(rows_v[...], gate_ref[:, cut], preferred_element_type=jnp.float32)
        up = jnp.dot(rows_v[...], up_ref[:, cut], preferred_element_type=jnp.float32)
        act_v[:, cut] = (gate / (1.0 + jnp.exp(-gate)) * up).astype(jnp.bfloat16)
    for cut in down_cuts:
        produced = jnp.dot(act_v[...], down_ref[:, cut], preferred_element_type=jnp.float32)
        out_here[:, cut] = (weight_here * produced[:half]).astype(jnp.bfloat16)
        out_there[:, cut] = (weight_there * produced[half:]).astype(jnp.bfloat16)


def expert_piece(here, there, experts, pieces, after=()):
    half = here.shape[0]
    hidden, width = pieces[2].shape
    out = pltpu.VMEM((half, width), jnp.bfloat16)
    vmem = whole(pltpu.VMEM)
    return pl.pallas_call(
        functools.partial(experts_kernel, experts, len(after)),
        out_shape=(out, out),
        in_specs=[vmem] * 5 + [whole(pl.ANY)] * len(after),
        out_specs=(vmem, vmem),
        scratch_shapes=[
            pltpu.VMEM((2 * half, width), jnp.bfloat16),
            pltpu.VMEM((2 * half, hidden), jnp.bfloat16),
        ],
        compiler_params=pltpu.CompilerParams(vmem_limit_bytes=64 * half * 1024 + 4 * MIB),
        cost_estimate=pl.CostEstimate(
            flops=12 * half * width * hidden, bytes_accessed=0, transcendentals=2 * half * hidden
        ),
        name="expert_piece",
    )(here, there, *pieces, *after)


def exchange(rows, node_mask, local_mask):
    nodes = lax.axis_size("node")
    locals_ = lax.axis_size("local")
    pairs = [
        (n * locals_ + k, (n ^ node_mask) * locals_ + (k ^ local_mask))
        for n in range(nodes)
        for k in range(locals_)
    ]
    return lax.ppermute(rows, ("node", "local"), pairs)


def masks():
    locals_, nodes = lax.axis_size("local"), lax.axis_size("node")
    near, far = list(range(locals_ // 2)), list(range(locals_ // 2, locals_))
    return near, far, [nodes - 2] + list(range(2, nodes - 2, 2))


def gather_plane(line, after=()):
    return pack([line] + [exchange(line, n, 0) for n in masks()[2]], after=after)


def f32(x):
    return x.astype(jnp.float32)


def block(x, size, i):
    return x[i * size : (i + 1) * size]


def core_sum(here, there):
    return f32(here) + f32(exchange(there, 1, 0))


def plane_sum(sums):
    plane = masks()[2]
    size = sums.shape[0] // (1 + len(plane))
    line, packed = sums[:size], sums.astype(jnp.bfloat16)
    for i, n in enumerate(plane):
        line = line + f32(exchange(block(packed, size, i + 1), n, 0))
    return line


def per_device(
    queries,
    key_cache,
    value_cache,
    fresh_token_keys,
    new_values,
    lengths,
    hidden_rows,
    norm_gain,
    expert_ids,
    route_scores,
    gate_weight,
    up_weight,
    down_weight,
):
    context = attend(queries, key_cache, value_cache, fresh_token_keys, new_values, lengths)
    experts = lax.axis_size("node") * lax.axis_size("local") // 2
    count = hidden_rows.shape[0]
    near, far, _ = masks()
    rows = prepare(hidden_rows, norm_gain, expert_ids, route_scores, experts)
    line = {k: exchange(rows, 0, k) for k in near[1:] + far}
    second = pack([line[k] for k in far], after=(in_hbm(context),))
    first = gather_plane(pack([rows] + [line[k] for k in near[1:]]), after=(second,))
    pieces = (gate_weight[0], up_weight[0], down_weight[0])
    first, first_other = expert_piece(first, exchange(first, 1, 0), experts, pieces)
    second = gather_plane(second, after=(first,))
    second, first_other = lax.optimization_barrier((second, first_other))
    second, second_other = expert_piece(
        second, exchange(second, 1, 0), experts, pieces
    )
    line = plane_sum(core_sum(first, first_other))
    total, packed = line[:count], line.astype(jnp.bfloat16)
    line = plane_sum(core_sum(second, second_other)).astype(jnp.bfloat16)
    for i, k in enumerate(far):
        total = total + f32(exchange(block(line, count, i), 0, k))
    for i, k in enumerate(near[1:]):
        total = total + f32(exchange(block(packed, count, i + 1), 0, k))
    total = total.astype(jnp.bfloat16)
    return (context, total)


def solution(mesh):
    placed = (
        P(("group", "node", "local"), None, None),
        P(("group", "node", "local"), None, None, None),
        P(("group", "node", "local"), None, None, None),
        P(("group", "node", "local"), None, None),
        P(("group", "node", "local"), None, None),
        P(("group", "node", "local")),
        P(("group", "node", "local"), None),
        P(),
        P(("group", "node", "local"), None),
        P(("group", "node", "local"), None),
        P(("node", "local"), None, None),
        P(("node", "local"), None, None),
        P(("node", "local"), None, None),
    )
    return jax.shard_map(
        per_device,
        mesh=mesh,
        in_specs=placed,
        out_specs=(P(("group", "node", "local"), None), P(("group", "node", "local"), None)),
        check_vma=False,
    )
```

```python
import functools
import math

import jax
import jax.numpy as jnp
from jax import lax
from jax.experimental import pallas as pl
from jax.experimental.pallas import tpu as pltpu
from jax.sharding import PartitionSpec as P


MIB = 1024 * 1024
TILE = 256
DOWN_TILE = 1024
ATTEND_LIMIT = 12 * MIB


def whole(space):
    return pl.BlockSpec(memory_space=space)


def in_hbm(array):
    return pltpu.with_memory_space_constraint(array, pltpu.HBM)


def prepare_kernel(
    experts, hidden_hbm, gain_hbm, ids_hbm, scores_hbm, out_ref, hidden_ref, gain_ref, ids_ref, scores_ref, sems
):
    pairs = ((hidden_hbm, hidden_ref), (gain_hbm, gain_ref), (ids_hbm, ids_ref), (scores_hbm, scores_ref))
    copies = [pltpu.make_async_copy(a, b, sems.at[n]) for n, (a, b) in enumerate(pairs)]
    for copy in copies:
        copy.start()
    for copy in copies:
        copy.wait()
    width = hidden_ref.shape[1]
    hidden = hidden_ref[...].astype(jnp.float32)
    mean_square = jnp.mean(hidden * hidden, axis=1, keepdims=True)
    gain = gain_ref[...].astype(jnp.float32).reshape(1, width)
    out_ref[:, :width] = (hidden * lax.rsqrt(mean_square + 1e-06) * gain).astype(jnp.bfloat16)
    scores = scores_ref[...]
    gates = scores / jnp.sum(scores, axis=1, keepdims=True)
    ids = ids_ref[...]
    rows, extra = out_ref.shape[0], out_ref.shape[1] - width
    column = lax.broadcasted_iota(jnp.int32, (rows, extra), 1)
    expert = jnp.where(column < experts, column, column - experts)
    table = jnp.zeros((rows, extra), jnp.float32)
    for j in range(ids.shape[1]):
        table = table + jnp.where(ids[:, j : j + 1] == expert, gates[:, j : j + 1], 0.0)
    coarse = table.astype(jnp.bfloat16).astype(jnp.float32)
    parts = jnp.where(column < experts, coarse, jnp.where(column < 2 * experts, table - coarse, 0.0))
    out_ref[:, width:] = parts.astype(jnp.bfloat16)


def prepare(hidden_rows, norm_gain, expert_ids, route_scores, experts):
    rows, width = hidden_rows.shape
    extra = -(-2 * experts // 128) * 128
    args = (hidden_rows, norm_gain, expert_ids, route_scores)
    return pl.pallas_call(
        functools.partial(prepare_kernel, experts),
        out_shape=pltpu.VMEM((rows, width + extra), jnp.bfloat16),
        in_specs=[whole(pltpu.HBM)] * 4,
        out_specs=whole(pltpu.VMEM),
        scratch_shapes=[pltpu.VMEM(a.shape, a.dtype) for a in args] + [pltpu.SemaphoreType.DMA((4,))],
        compiler_params=pltpu.CompilerParams(vmem_limit_bytes=2 * MIB),
        name="prepare",
    )(*[in_hbm(a) for a in args])


def attend_kernel(
    kv_heads,
    inverse_scale,
    lengths_hbm,
    queries_hbm,
    keys_hbm,
    values_hbm,
    fresh_hbm,
    new_hbm,
    out_ref,
    lengths_ref,
    queries_v,
    keys_v,
    values_v,
    fresh_v,
    new_v,
    mixed_v,
    sems,
):
    requests, slots, width = keys_hbm.shape
    context = slots // kv_heads
    heads = queries_hbm.shape[1]
    group = heads // kv_heads
    pairs = [
        (queries_hbm, queries_v),
        (keys_hbm, keys_v.at[:, pl.ds(0, slots), :]),
        (values_hbm, values_v.at[:, pl.ds(0, slots), :]),
        (fresh_hbm, fresh_v),
        (new_hbm, new_v),
        (lengths_hbm, lengths_ref),
    ]
    copies = [pltpu.make_async_copy(a, b, sems.at[n]) for n, (a, b) in enumerate(pairs)]
    for copy in copies:
        copy.start()
    total = keys_v.shape[1]
    row_group = lax.broadcasted_iota(jnp.int32, (heads, total), 0) // group
    slot = lax.broadcasted_iota(jnp.int32, (heads, total), 1)
    offset = slot - row_group * context
    is_new = slot == slots + row_group
    empty = jnp.zeros((total - slots - kv_heads, width), jnp.float32)
    for copy in copies:
        copy.wait()
    for b in range(requests):
        for cache, token in ((keys_v, fresh_v), (values_v, new_v)):
            tail = jnp.concatenate([token[b].astype(jnp.float32), empty])
            cache[b, slots:, :] = tail.astype(jnp.bfloat16)
    scores = [
        lax.dot_general(
            queries_v[b], keys_v[b], (((1,), (1,)), ((), ())), preferred_element_type=jnp.float32
        )
        for b in range(requests)
    ]
    probs = []
    for b in range(requests):
        valid = (offset >= 0) & (offset < lengths_ref[b]) & (slot < slots) | is_new
        score = jnp.where(valid, scores[b] * inverse_scale, -1e30)
        exponent = jnp.exp(score - jnp.max(score, axis=1, keepdims=True))
        probs.append((exponent / jnp.sum(exponent, axis=1, keepdims=True)).astype(jnp.bfloat16))
    for b in range(requests):
        mixed_v[b * heads : (b + 1) * heads, :] = jnp.dot(
            probs[b], values_v[b], preferred_element_type=jnp.float32
        )
    for h in range(heads):
        rows = mixed_v[pl.ds(h, requests, stride=heads), :]
        out_ref[:, h * width : (h + 1) * width] = rows.astype(jnp.bfloat16)


def attend(queries, key_cache, value_cache, fresh_token_keys, new_values, lengths):
    requests, heads, width = queries.shape
    kv_heads, context = key_cache.shape[1:3]
    slots = kv_heads * context
    total = -(-(slots + kv_heads) // 128) * 128
    cache = pltpu.VMEM((requests, total, width), jnp.bfloat16)
    token = pltpu.VMEM(fresh_token_keys.shape, jnp.bfloat16)
    vmem = whole(pltpu.VMEM)
    return pl.pallas_call(
        functools.partial(attend_kernel, kv_heads, 1.0 / math.sqrt(width)),
        out_shape=jax.ShapeDtypeStruct((requests, heads * width), jnp.bfloat16),
        in_specs=[whole(pltpu.HBM)] * 6,
        out_specs=vmem,
        scratch_shapes=[
            pltpu.SMEM(lengths.shape, jnp.int32),
            pltpu.VMEM(queries.shape, jnp.bfloat16),
            cache,
            cache,
            token,
            token,
            pltpu.VMEM((requests * heads, width), jnp.float32),
            pltpu.SemaphoreType.DMA((6,)),
        ],
        compiler_params=pltpu.CompilerParams(vmem_limit_bytes=ATTEND_LIMIT),
        cost_estimate=pl.CostEstimate(
            flops=12 * 10**9,
            bytes_accessed=4 * key_cache.size,
            transcendentals=requests * heads * total,
        ),
        name="attend",
    )(
        in_hbm(lengths),
        in_hbm(queries),
        in_hbm(key_cache.reshape(requests, slots, width)),
        in_hbm(value_cache.reshape(requests, slots, width)),
        in_hbm(fresh_token_keys),
        in_hbm(new_values),
    )


def pack_kernel(tail, after, *refs):
    refs = refs[after:]
    out_ref, tail_ref = refs[-2:] if tail else (refs[-1], None)
    refs = refs[: -2 if tail else -1]
    start, inner = 0, 0
    for n, ref in enumerate(refs):
        out_ref[start : start + ref.shape[0], :] = ref[...]
        start += ref.shape[0]
        if n >= len(refs) - tail:
            tail_ref[inner : inner + ref.shape[0], :] = ref[...]
            inner += ref.shape[0]


def pack(pieces, tail=0, after=()):
    width, dtype = pieces[0].shape[1], pieces[0].dtype

    def out(pieces):
        return pltpu.VMEM((sum(piece.shape[0] for piece in pieces), width), dtype)

    vmem = whole(pltpu.VMEM)
    return pl.pallas_call(
        functools.partial(pack_kernel, tail, len(after)),
        out_shape=(out(pieces), out(pieces[-tail:])) if tail else out(pieces),
        in_specs=[whole(pl.ANY)] * len(after) + [vmem] * len(pieces),
        out_specs=(vmem, vmem) if tail else vmem,
        compiler_params=pltpu.CompilerParams(vmem_limit_bytes=MIB),
        name="pack",
    )(*after, *pieces)


def experts_kernel(
    experts, after, here_ref, there_ref, gate_ref, up_ref, down_ref, *refs
):
    out_here, out_there, rows_v, act_v = refs[after:]
    hidden, width = down_ref.shape
    cuts = [pl.ds(t, TILE) for t in range(0, hidden, TILE)]
    down_cuts = [pl.ds(t, DOWN_TILE) for t in range(0, width, DOWN_TILE)]
    half = here_ref.shape[0]
    rows_v[:half, :] = here_ref[:, :width]
    rows_v[half:, :] = there_ref[:, :width]
    column = lax.broadcasted_iota(jnp.int32, (1, here_ref.shape[1] - width), 1)
    own = (lax.axis_index("node") * lax.axis_size("local") + lax.axis_index("local")) // 2
    mine = (column == own) | (column == own + experts)

    def weights_of(ref):
        parts = jnp.where(mine, ref[:, width:].astype(jnp.float32), 0.0)
        return jnp.sum(parts, axis=1, keepdims=True)

    weight_here, weight_there = weights_of(here_ref), weights_of(there_ref)
    for cut in cuts:
        gate = jnp.dot(rows_v[...], gate_ref[:, cut], preferred_element_type=jnp.float32)
        up = jnp.dot(rows_v[...], up_ref[:, cut], preferred_element_type=jnp.float32)
        act_v[:, cut] = (gate / (1.0 + jnp.exp(-gate)) * up).astype(jnp.bfloat16)
    for cut in down_cuts:
        produced = jnp.dot(act_v[...], down_ref[:, cut], preferred_element_type=jnp.float32)
        out_here[:, cut] = (weight_here * produced[:half]).astype(jnp.bfloat16)
        out_there[:, cut] = (weight_there * produced[half:]).astype(jnp.bfloat16)


def expert_piece(here, there, experts, pieces, after=()):
    half = here.shape[0]
    hidden, width = pieces[2].shape
    out = pltpu.VMEM((half, width), jnp.bfloat16)
    vmem = whole(pltpu.VMEM)
    return pl.pallas_call(
        functools.partial(experts_kernel, experts, len(after)),
        out_shape=(out, out),
        in_specs=[vmem] * 5 + [whole(pl.ANY)] * len(after),
        out_specs=(vmem, vmem),
        scratch_shapes=[
            pltpu.VMEM((2 * half, width), jnp.bfloat16),
            pltpu.VMEM((2 * half, hidden), jnp.bfloat16),
        ],
        compiler_params=pltpu.CompilerParams(vmem_limit_bytes=64 * half * 1024 + 4 * MIB),
        cost_estimate=pl.CostEstimate(
            flops=12 * half * width * hidden, bytes_accessed=0, transcendentals=2 * half * hidden
        ),
        name="expert_piece",
    )(here, there, *pieces, *after)


def exchange(rows, node_mask, local_mask):
    nodes = lax.axis_size("node")
    locals_ = lax.axis_size("local")
    pairs = [
        (n * locals_ + k, (n ^ node_mask) * locals_ + (k ^ local_mask))
        for n in range(nodes)
        for k in range(locals_)
    ]
    return lax.ppermute(rows, ("node", "local"), pairs)


def masks():
    locals_, nodes = lax.axis_size("local"), lax.axis_size("node")
    near, far = list(range(locals_ // 2)), list(range(locals_ // 2, locals_))
    return near, far, [nodes - 2] + list(range(2, nodes - 2, 2))


def gather_plane(line, after=()):
    return pack([line] + [exchange(line, n, 0) for n in masks()[2]], after=after)


def f32(x):
    return x.astype(jnp.float32)


def block(x, size, i):
    return x[i * size : (i + 1) * size]


def core_sum(here, there):
    return f32(here) + f32(exchange(there, 1, 0))


def plane_sum(sums):
    plane = masks()[2]
    size = sums.shape[0] // (1 + len(plane))
    line, packed = sums[:size], sums.astype(jnp.bfloat16)
    for i, n in enumerate(plane):
        line = line + f32(exchange(block(packed, size, i + 1), n, 0))
    return line


def per_device(
    queries,
    key_cache,
    value_cache,
    fresh_token_keys,
    new_values,
    lengths,
    hidden_rows,
    norm_gain,
    expert_ids,
    route_scores,
    gate_weight,
    up_weight,
    down_weight,
):
    context = attend(queries, key_cache, value_cache, fresh_token_keys, new_values, lengths)
    experts = lax.axis_size("node") * lax.axis_size("local") // 2
    count = hidden_rows.shape[0]
    near, far, _ = masks()
    rows = prepare(hidden_rows, norm_gain, expert_ids, route_scores, experts)
    line = {k: exchange(rows, 0, k) for k in near[1:] + far}
    second = pack([line[k] for k in far], after=(in_hbm(context),))
    first = gather_plane(pack([rows] + [line[k] for k in near[1:]]), after=(second,))
    pieces = (gate_weight[0], up_weight[0], down_weight[0])
    first, first_other = expert_piece(first, exchange(first, 1, 0), experts, pieces)
    second = gather_plane(second)
    second_other = exchange(second, 1, 0)
    second, second_other = expert_piece(second, second_other, experts, pieces, (first,))
    plane = masks()[2]
    sums = core_sum(second, second_other)
    size = sums.shape[0] // (1 + len(plane))
    packed, farther = sums.astype(jnp.bfloat16), sums[:size]
    arrived = [exchange(block(packed, size, i + 1), n, 0) for i, n in enumerate(plane)]
    arrived[1], nearer = lax.optimization_barrier((arrived[1], core_sum(first, first_other)))
    for piece in arrived:
        farther = farther + f32(piece)
    farther = farther.astype(jnp.bfloat16)
    nearer = plane_sum(nearer)
    total, packed = nearer[:count], nearer.astype(jnp.bfloat16)
    for i, k in enumerate(far):
        total = total + f32(exchange(block(farther, count, i), 0, k))
    for i, k in enumerate(near[1:]):
        total = total + f32(exchange(block(packed, count, i + 1), 0, k))
    total = total.astype(jnp.bfloat16)
    return (context, total)


def solution(mesh):
    placed = (
        P(("group", "node", "local"), None, None),
        P(("group", "node", "local"), None, None, None),
        P(("group", "node", "local"), None, None, None),
        P(("group", "node", "local"), None, None),
        P(("group", "node", "local"), None, None),
        P(("group", "node", "local")),
        P(("group", "node", "local"), None),
        P(),
        P(("group", "node", "local"), None),
        P(("group", "node", "local"), None),
        P(("node", "local"), None, None),
        P(("node", "local"), None, None),
        P(("node", "local"), None, None),
    )
    return jax.shard_map(
        per_device,
        mesh=mesh,
        in_specs=placed,
        out_specs=(P(("group", "node", "local"), None), P(("group", "node", "local"), None)),
        check_vma=False,
    )
```

```python
import functools
import math

import jax
import jax.numpy as jnp
from jax import lax
from jax.experimental import pallas as pl
from jax.experimental.pallas import tpu as pltpu
from jax.sharding import PartitionSpec as P


MIB = 1024 * 1024
TILE = 256
DOWN_TILE = 1024
ATTEND_LIMIT = 12 * MIB


def whole(space):
    return pl.BlockSpec(memory_space=space)


def in_hbm(array):
    return pltpu.with_memory_space_constraint(array, pltpu.HBM)


def prepare_kernel(
    experts, hidden_hbm, gain_hbm, ids_hbm, scores_hbm, out_ref, hidden_ref, gain_ref, ids_ref, scores_ref, sems
):
    pairs = ((hidden_hbm, hidden_ref), (gain_hbm, gain_ref), (ids_hbm, ids_ref), (scores_hbm, scores_ref))
    copies = [pltpu.make_async_copy(a, b, sems.at[n]) for n, (a, b) in enumerate(pairs)]
    for copy in copies:
        copy.start()
    for copy in copies:
        copy.wait()
    width = hidden_ref.shape[1]
    hidden = hidden_ref[...].astype(jnp.float32)
    mean_square = jnp.mean(hidden * hidden, axis=1, keepdims=True)
    gain = gain_ref[...].astype(jnp.float32).reshape(1, width)
    out_ref[:, :width] = (hidden * lax.rsqrt(mean_square + 1e-06) * gain).astype(jnp.bfloat16)
    scores = scores_ref[...]
    gates = scores / jnp.sum(scores, axis=1, keepdims=True)
    ids = ids_ref[...]
    rows, extra = out_ref.shape[0], out_ref.shape[1] - width
    column = lax.broadcasted_iota(jnp.int32, (rows, extra), 1)
    expert = jnp.where(column < experts, column, column - experts)
    table = jnp.zeros((rows, extra), jnp.float32)
    for j in range(ids.shape[1]):
        table = table + jnp.where(ids[:, j : j + 1] == expert, gates[:, j : j + 1], 0.0)
    coarse = table.astype(jnp.bfloat16).astype(jnp.float32)
    parts = jnp.where(column < experts, coarse, jnp.where(column < 2 * experts, table - coarse, 0.0))
    out_ref[:, width:] = parts.astype(jnp.bfloat16)


def prepare(hidden_rows, norm_gain, expert_ids, route_scores, experts):
    rows, width = hidden_rows.shape
    extra = -(-2 * experts // 128) * 128
    args = (hidden_rows, norm_gain, expert_ids, route_scores)
    return pl.pallas_call(
        functools.partial(prepare_kernel, experts),
        out_shape=pltpu.VMEM((rows, width + extra), jnp.bfloat16),
        in_specs=[whole(pltpu.HBM)] * 4,
        out_specs=whole(pltpu.VMEM),
        scratch_shapes=[pltpu.VMEM(a.shape, a.dtype) for a in args] + [pltpu.SemaphoreType.DMA((4,))],
        compiler_params=pltpu.CompilerParams(vmem_limit_bytes=2 * MIB),
        name="prepare",
    )(*[in_hbm(a) for a in args])


def attend_kernel(
    kv_heads,
    inverse_scale,
    lengths_hbm,
    queries_hbm,
    keys_hbm,
    values_hbm,
    fresh_hbm,
    new_hbm,
    out_ref,
    lengths_ref,
    queries_v,
    keys_v,
    values_v,
    fresh_v,
    new_v,
    mixed_v,
    sems,
):
    requests, slots, width = keys_hbm.shape
    context = slots // kv_heads
    heads = queries_hbm.shape[1]
    group = heads // kv_heads
    pairs = [
        (queries_hbm, queries_v),
        (keys_hbm, keys_v.at[:, pl.ds(0, slots), :]),
        (values_hbm, values_v.at[:, pl.ds(0, slots), :]),
        (fresh_hbm, fresh_v),
        (new_hbm, new_v),
        (lengths_hbm, lengths_ref),
    ]
    copies = [pltpu.make_async_copy(a, b, sems.at[n]) for n, (a, b) in enumerate(pairs)]
    for copy in copies:
        copy.start()
    total = keys_v.shape[1]
    row_group = lax.broadcasted_iota(jnp.int32, (heads, total), 0) // group
    slot = lax.broadcasted_iota(jnp.int32, (heads, total), 1)
    offset = slot - row_group * context
    is_new = slot == slots + row_group
    empty = jnp.zeros((total - slots - kv_heads, width), jnp.float32)
    for copy in copies:
        copy.wait()
    for b in range(requests):
        for cache, token in ((keys_v, fresh_v), (values_v, new_v)):
            tail = jnp.concatenate([token[b].astype(jnp.float32), empty])
            cache[b, slots:, :] = tail.astype(jnp.bfloat16)
    scores = [
        lax.dot_general(
            queries_v[b], keys_v[b], (((1,), (1,)), ((), ())), preferred_element_type=jnp.float32
        )
        for b in range(requests)
    ]
    probs = []
    for b in range(requests):
        valid = (offset >= 0) & (offset < lengths_ref[b]) & (slot < slots) | is_new
        score = jnp.where(valid, scores[b] * inverse_scale, -1e30)
        exponent = jnp.exp(score - jnp.max(score, axis=1, keepdims=True))
        probs.append((exponent / jnp.sum(exponent, axis=1, keepdims=True)).astype(jnp.bfloat16))
    for b in range(requests):
        mixed_v[b * heads : (b + 1) * heads, :] = jnp.dot(
            probs[b], values_v[b], preferred_element_type=jnp.float32
        )
    for h in range(heads):
        rows = mixed_v[pl.ds(h, requests, stride=heads), :]
        out_ref[:, h * width : (h + 1) * width] = rows.astype(jnp.bfloat16)


def attend(queries, key_cache, value_cache, fresh_token_keys, new_values, lengths):
    requests, heads, width = queries.shape
    kv_heads, context = key_cache.shape[1:3]
    slots = kv_heads * context
    total = -(-(slots + kv_heads) // 128) * 128
    cache = pltpu.VMEM((requests, total, width), jnp.bfloat16)
    token = pltpu.VMEM(fresh_token_keys.shape, jnp.bfloat16)
    vmem = whole(pltpu.VMEM)
    return pl.pallas_call(
        functools.partial(attend_kernel, kv_heads, 1.0 / math.sqrt(width)),
        out_shape=jax.ShapeDtypeStruct((requests, heads * width), jnp.bfloat16),
        in_specs=[whole(pltpu.HBM)] * 6,
        out_specs=vmem,
        scratch_shapes=[
            pltpu.SMEM(lengths.shape, jnp.int32),
            pltpu.VMEM(queries.shape, jnp.bfloat16),
            cache,
            cache,
            token,
            token,
            pltpu.VMEM((requests * heads, width), jnp.float32),
            pltpu.SemaphoreType.DMA((6,)),
        ],
        compiler_params=pltpu.CompilerParams(vmem_limit_bytes=ATTEND_LIMIT),
        cost_estimate=pl.CostEstimate(
            flops=12 * 10**9,
            bytes_accessed=4 * key_cache.size,
            transcendentals=requests * heads * total,
        ),
        name="attend",
    )(
        in_hbm(lengths),
        in_hbm(queries),
        in_hbm(key_cache.reshape(requests, slots, width)),
        in_hbm(value_cache.reshape(requests, slots, width)),
        in_hbm(fresh_token_keys),
        in_hbm(new_values),
    )


def pack_kernel(tail, after, *refs):
    refs = refs[after:]
    out_ref, tail_ref = refs[-2:] if tail else (refs[-1], None)
    refs = refs[: -2 if tail else -1]
    start, inner = 0, 0
    for n, ref in enumerate(refs):
        out_ref[start : start + ref.shape[0], :] = ref[...]
        start += ref.shape[0]
        if n >= len(refs) - tail:
            tail_ref[inner : inner + ref.shape[0], :] = ref[...]
            inner += ref.shape[0]


def pack(pieces, tail=0, after=()):
    width, dtype = pieces[0].shape[1], pieces[0].dtype

    def out(pieces):
        return pltpu.VMEM((sum(piece.shape[0] for piece in pieces), width), dtype)

    vmem = whole(pltpu.VMEM)
    return pl.pallas_call(
        functools.partial(pack_kernel, tail, len(after)),
        out_shape=(out(pieces), out(pieces[-tail:])) if tail else out(pieces),
        in_specs=[whole(pl.ANY)] * len(after) + [vmem] * len(pieces),
        out_specs=(vmem, vmem) if tail else vmem,
        compiler_params=pltpu.CompilerParams(vmem_limit_bytes=MIB),
        name="pack",
    )(*after, *pieces)


def experts_kernel(
    experts, after, here_ref, there_ref, gate_ref, up_ref, down_ref, *refs
):
    out_here, out_there, rows_v, act_v = refs[after:]
    hidden, width = down_ref.shape
    cuts = [pl.ds(t, TILE) for t in range(0, hidden, TILE)]
    down_cuts = [pl.ds(t, DOWN_TILE) for t in range(0, width, DOWN_TILE)]
    half = here_ref.shape[0]
    rows_v[:half, :] = here_ref[:, :width]
    rows_v[half:, :] = there_ref[:, :width]
    column = lax.broadcasted_iota(jnp.int32, (1, here_ref.shape[1] - width), 1)
    own = (lax.axis_index("node") * lax.axis_size("local") + lax.axis_index("local")) // 2
    mine = (column == own) | (column == own + experts)

    def weights_of(ref):
        parts = jnp.where(mine, ref[:, width:].astype(jnp.float32), 0.0)
        return jnp.sum(parts, axis=1, keepdims=True)

    weight_here, weight_there = weights_of(here_ref), weights_of(there_ref)
    for cut in cuts:
        gate = jnp.dot(rows_v[...], gate_ref[:, cut], preferred_element_type=jnp.float32)
        up = jnp.dot(rows_v[...], up_ref[:, cut], preferred_element_type=jnp.float32)
        act_v[:, cut] = (gate / (1.0 + jnp.exp(-gate)) * up).astype(jnp.bfloat16)
    for cut in down_cuts:
        produced = jnp.dot(act_v[...], down_ref[:, cut], preferred_element_type=jnp.float32)
        out_here[:, cut] = (weight_here * produced[:half]).astype(jnp.bfloat16)
        out_there[:, cut] = (weight_there * produced[half:]).astype(jnp.bfloat16)


def expert_piece(here, there, experts, pieces, after=()):
    half = here.shape[0]
    hidden, width = pieces[2].shape
    out = pltpu.VMEM((half, width), jnp.bfloat16)
    vmem = whole(pltpu.VMEM)
    return pl.pallas_call(
        functools.partial(experts_kernel, experts, len(after)),
        out_shape=(out, out),
        in_specs=[vmem] * 5 + [whole(pl.ANY)] * len(after),
        out_specs=(vmem, vmem),
        scratch_shapes=[
            pltpu.VMEM((2 * half, width), jnp.bfloat16),
            pltpu.VMEM((2 * half, hidden), jnp.bfloat16),
        ],
        compiler_params=pltpu.CompilerParams(vmem_limit_bytes=64 * half * 1024 + 4 * MIB),
        cost_estimate=pl.CostEstimate(
            flops=12 * half * width * hidden, bytes_accessed=0, transcendentals=2 * half * hidden
        ),
        name="expert_piece",
    )(here, there, *pieces, *after)


def exchange(rows, node_mask, local_mask):
    nodes = lax.axis_size("node")
    locals_ = lax.axis_size("local")
    pairs = [
        (n * locals_ + k, (n ^ node_mask) * locals_ + (k ^ local_mask))
        for n in range(nodes)
        for k in range(locals_)
    ]
    return lax.ppermute(rows, ("node", "local"), pairs)


def masks():
    locals_, nodes = lax.axis_size("local"), lax.axis_size("node")
    near, far = list(range(locals_ // 2)), list(range(locals_ // 2, locals_))
    return near, far, list(range(nodes - 4, 0, -2)) + [nodes - 2]


def gather_plane(line, after=()):
    return pack([line] + [exchange(line, n, 0) for n in masks()[2]], after=after)


def f32(x):
    return x.astype(jnp.float32)


def block(x, size, i):
    return x[i * size : (i + 1) * size]


def core_sum(here, there):
    return f32(here) + f32(exchange(there, 1, 0))


def plane_sum(sums):
    plane = masks()[2]
    size = sums.shape[0] // (1 + len(plane))
    line, packed = sums[:size], sums.astype(jnp.bfloat16)
    for i, n in enumerate(plane):
        line = line + f32(exchange(block(packed, size, i + 1), n, 0))
    return line


def per_device(
    queries,
    key_cache,
    value_cache,
    fresh_token_keys,
    new_values,
    lengths,
    hidden_rows,
    norm_gain,
    expert_ids,
    route_scores,
    gate_weight,
    up_weight,
    down_weight,
):
    context = attend(queries, key_cache, value_cache, fresh_token_keys, new_values, lengths)
    experts = lax.axis_size("node") * lax.axis_size("local") // 2
    count = hidden_rows.shape[0]
    near, far, _ = masks()
    rows = prepare(hidden_rows, norm_gain, expert_ids, route_scores, experts)
    line = {k: exchange(rows, 0, k) for k in near[1:] + far}
    second = pack([line[k] for k in far], after=(in_hbm(context),))
    first = gather_plane(pack([rows] + [line[k] for k in near[1:]]), after=(second,))
    pieces = (gate_weight[0], up_weight[0], down_weight[0])
    first, first_other = expert_piece(first, exchange(first, 1, 0), experts, pieces)
    second = gather_plane(second, after=(first,))
    second, first_other = lax.optimization_barrier((second, first_other))
    second, second_other = expert_piece(second, exchange(second, 1, 0), experts, pieces)
    plane = masks()[2]
    sums = core_sum(second, second_other)
    size = sums.shape[0] // (1 + len(plane))
    packed, farther = sums.astype(jnp.bfloat16), sums[:size]
    arrived = [exchange(block(packed, size, i + 1), n, 0) for i, n in enumerate(plane)]
    arrived[0], nearer = lax.optimization_barrier((arrived[0], core_sum(first, first_other)))
    for piece in arrived:
        farther = farther + f32(piece)
    farther = farther.astype(jnp.bfloat16)
    nearer = plane_sum(nearer)
    total, packed = nearer[:count], nearer.astype(jnp.bfloat16)
    for i, k in enumerate(far):
        total = total + f32(exchange(block(farther, count, i), 0, k))
    for i, k in enumerate(near[1:]):
        total = total + f32(exchange(block(packed, count, i + 1), 0, k))
    total = total.astype(jnp.bfloat16)
    return (context, total)


def solution(mesh):
    placed = (
        P(("group", "node", "local"), None, None),
        P(("group", "node", "local"), None, None, None),
        P(("group", "node", "local"), None, None, None),
        P(("group", "node", "local"), None, None),
        P(("group", "node", "local"), None, None),
        P(("group", "node", "local")),
        P(("group", "node", "local"), None),
        P(),
        P(("group", "node", "local"), None),
        P(("group", "node", "local"), None),
        P(("node", "local"), None, None),
        P(("node", "local"), None, None),
        P(("node", "local"), None, None),
    )
    return jax.shard_map(
        per_device,
        mesh=mesh,
        in_specs=placed,
        out_specs=(P(("group", "node", "local"), None), P(("group", "node", "local"), None)),
        check_vma=False,
    )
```

```python
import functools
import math

import jax
import jax.numpy as jnp
from jax import lax
from jax.experimental import pallas as pl
from jax.experimental.pallas import tpu as pltpu
from jax.sharding import PartitionSpec as P


MIB = 1024 * 1024
TILE = 768
DOWN_TILE = 4096
ATTEND_LIMIT = 12 * MIB


def whole(space):
    return pl.BlockSpec(memory_space=space)


def in_hbm(array):
    return pltpu.with_memory_space_constraint(array, pltpu.HBM)


def prepare_kernel(
    experts, hidden_hbm, gain_hbm, ids_hbm, scores_hbm, out_ref, hidden_ref, gain_ref, ids_ref, scores_ref, sems
):
    pairs = ((hidden_hbm, hidden_ref), (gain_hbm, gain_ref), (ids_hbm, ids_ref), (scores_hbm, scores_ref))
    copies = [pltpu.make_async_copy(a, b, sems.at[n]) for n, (a, b) in enumerate(pairs)]
    for copy in copies:
        copy.start()
    for copy in copies:
        copy.wait()
    width = hidden_ref.shape[1]
    hidden = hidden_ref[...].astype(jnp.float32)
    mean_square = jnp.mean(hidden * hidden, axis=1, keepdims=True)
    gain = gain_ref[...].astype(jnp.float32).reshape(1, width)
    out_ref[:, :width] = (hidden * lax.rsqrt(mean_square + 1e-06) * gain).astype(jnp.bfloat16)
    scores = scores_ref[...]
    gates = scores / jnp.sum(scores, axis=1, keepdims=True)
    ids = ids_ref[...]
    rows, extra = out_ref.shape[0], out_ref.shape[1] - width
    column = lax.broadcasted_iota(jnp.int32, (rows, extra), 1)
    expert = jnp.where(column < experts, column, column - experts)
    table = jnp.zeros((rows, extra), jnp.float32)
    for j in range(ids.shape[1]):
        table = table + jnp.where(ids[:, j : j + 1] == expert, gates[:, j : j + 1], 0.0)
    coarse = table.astype(jnp.bfloat16).astype(jnp.float32)
    parts = jnp.where(column < experts, coarse, jnp.where(column < 2 * experts, table - coarse, 0.0))
    out_ref[:, width:] = parts.astype(jnp.bfloat16)


def prepare(hidden_rows, norm_gain, expert_ids, route_scores, experts):
    rows, width = hidden_rows.shape
    extra = -(-2 * experts // 128) * 128
    args = (hidden_rows, norm_gain, expert_ids, route_scores)
    return pl.pallas_call(
        functools.partial(prepare_kernel, experts),
        out_shape=pltpu.VMEM((rows, width + extra), jnp.bfloat16),
        in_specs=[whole(pltpu.HBM)] * 4,
        out_specs=whole(pltpu.VMEM),
        scratch_shapes=[pltpu.VMEM(a.shape, a.dtype) for a in args] + [pltpu.SemaphoreType.DMA((4,))],
        compiler_params=pltpu.CompilerParams(vmem_limit_bytes=2 * MIB),
        name="prepare",
    )(*[in_hbm(a) for a in args])


def attend_kernel(
    kv_heads,
    inverse_scale,
    lengths_hbm,
    queries_hbm,
    keys_hbm,
    values_hbm,
    fresh_hbm,
    new_hbm,
    out_ref,
    lengths_ref,
    queries_v,
    keys_v,
    values_v,
    fresh_v,
    new_v,
    mixed_v,
    sems,
):
    requests, slots, width = keys_hbm.shape
    context = slots // kv_heads
    heads = queries_hbm.shape[1]
    group = heads // kv_heads
    pairs = [
        (queries_hbm, queries_v),
        (keys_hbm, keys_v.at[:, pl.ds(0, slots), :]),
        (values_hbm, values_v.at[:, pl.ds(0, slots), :]),
        (fresh_hbm, fresh_v),
        (new_hbm, new_v),
        (lengths_hbm, lengths_ref),
    ]
    copies = [pltpu.make_async_copy(a, b, sems.at[n]) for n, (a, b) in enumerate(pairs)]
    for copy in copies:
        copy.start()
    total = keys_v.shape[1]
    row_group = lax.broadcasted_iota(jnp.int32, (heads, total), 0) // group
    slot = lax.broadcasted_iota(jnp.int32, (heads, total), 1)
    offset = slot - row_group * context
    is_new = slot == slots + row_group
    empty = jnp.zeros((total - slots - kv_heads, width), jnp.float32)
    for copy in copies:
        copy.wait()
    for b in range(requests):
        for cache, token in ((keys_v, fresh_v), (values_v, new_v)):
            tail = jnp.concatenate([token[b].astype(jnp.float32), empty])
            cache[b, slots:, :] = tail.astype(jnp.bfloat16)
    scores = [
        lax.dot_general(
            queries_v[b], keys_v[b], (((1,), (1,)), ((), ())), preferred_element_type=jnp.float32
        )
        for b in range(requests)
    ]
    probs = []
    for b in range(requests):
        valid = (offset >= 0) & (offset < lengths_ref[b]) & (slot < slots) | is_new
        score = jnp.where(valid, scores[b] * inverse_scale, -1e30)
        exponent = jnp.exp(score - jnp.max(score, axis=1, keepdims=True))
        probs.append((exponent / jnp.sum(exponent, axis=1, keepdims=True)).astype(jnp.bfloat16))
    for b in range(requests):
        mixed_v[b * heads : (b + 1) * heads, :] = jnp.dot(
            probs[b], values_v[b], preferred_element_type=jnp.float32
        )
    for h in range(heads):
        rows = mixed_v[pl.ds(h, requests, stride=heads), :]
        out_ref[:, h * width : (h + 1) * width] = rows.astype(jnp.bfloat16)


def attend(queries, key_cache, value_cache, fresh_token_keys, new_values, lengths):
    requests, heads, width = queries.shape
    kv_heads, context = key_cache.shape[1:3]
    slots = kv_heads * context
    total = -(-(slots + kv_heads) // 128) * 128
    cache = pltpu.VMEM((requests, total, width), jnp.bfloat16)
    token = pltpu.VMEM(fresh_token_keys.shape, jnp.bfloat16)
    vmem = whole(pltpu.VMEM)
    return pl.pallas_call(
        functools.partial(attend_kernel, kv_heads, 1.0 / math.sqrt(width)),
        out_shape=jax.ShapeDtypeStruct((requests, heads * width), jnp.bfloat16),
        in_specs=[whole(pltpu.HBM)] * 6,
        out_specs=vmem,
        scratch_shapes=[
            pltpu.SMEM(lengths.shape, jnp.int32),
            pltpu.VMEM(queries.shape, jnp.bfloat16),
            cache,
            cache,
            token,
            token,
            pltpu.VMEM((requests * heads, width), jnp.float32),
            pltpu.SemaphoreType.DMA((6,)),
        ],
        compiler_params=pltpu.CompilerParams(vmem_limit_bytes=ATTEND_LIMIT),
        cost_estimate=pl.CostEstimate(
            flops=12 * 10**9,
            bytes_accessed=4 * key_cache.size,
            transcendentals=requests * heads * total,
        ),
        name="attend",
    )(
        in_hbm(lengths),
        in_hbm(queries),
        in_hbm(key_cache.reshape(requests, slots, width)),
        in_hbm(value_cache.reshape(requests, slots, width)),
        in_hbm(fresh_token_keys),
        in_hbm(new_values),
    )


def pack_kernel(tail, after, *refs):
    refs = refs[after:]
    out_ref, tail_ref = refs[-2:] if tail else (refs[-1], None)
    refs = refs[: -2 if tail else -1]
    start, inner = 0, 0
    for n, ref in enumerate(refs):
        out_ref[start : start + ref.shape[0], :] = ref[...]
        start += ref.shape[0]
        if n >= len(refs) - tail:
            tail_ref[inner : inner + ref.shape[0], :] = ref[...]
            inner += ref.shape[0]


def pack(pieces, tail=0, after=()):
    width, dtype = pieces[0].shape[1], pieces[0].dtype

    def out(pieces):
        return pltpu.VMEM((sum(piece.shape[0] for piece in pieces), width), dtype)

    vmem = whole(pltpu.VMEM)
    return pl.pallas_call(
        functools.partial(pack_kernel, tail, len(after)),
        out_shape=(out(pieces), out(pieces[-tail:])) if tail else out(pieces),
        in_specs=[whole(pl.ANY)] * len(after) + [vmem] * len(pieces),
        out_specs=(vmem, vmem) if tail else vmem,
        compiler_params=pltpu.CompilerParams(vmem_limit_bytes=MIB),
        name="pack",
    )(*after, *pieces)


def experts_kernel(
    experts, after, here_ref, there_ref, gate_ref, up_ref, down_ref, *refs
):
    out_here, out_there, rows_v, act_v = refs[after:]
    hidden, width = down_ref.shape
    cuts = [pl.ds(t, TILE) for t in range(0, hidden, TILE)]
    down_cuts = [pl.ds(t, DOWN_TILE) for t in range(0, width, DOWN_TILE)]
    half = here_ref.shape[0]
    rows_v[:half, :] = here_ref[:, :width]
    rows_v[half:, :] = there_ref[:, :width]
    column = lax.broadcasted_iota(jnp.int32, (1, here_ref.shape[1] - width), 1)
    own = (lax.axis_index("node") * lax.axis_size("local") + lax.axis_index("local")) // 2
    mine = (column == own) | (column == own + experts)

    def weights_of(ref):
        parts = jnp.where(mine, ref[:, width:].astype(jnp.float32), 0.0)
        return jnp.sum(parts, axis=1, keepdims=True)

    weight_here, weight_there = weights_of(here_ref), weights_of(there_ref)
    for cut in cuts:
        gate = jnp.dot(rows_v[...], gate_ref[:, cut], preferred_element_type=jnp.float32)
        up = jnp.dot(rows_v[...], up_ref[:, cut], preferred_element_type=jnp.float32)
        act_v[:, cut] = (gate / (1.0 + jnp.exp(-gate)) * up).astype(jnp.bfloat16)
    for cut in down_cuts:
        produced = jnp.dot(act_v[...], down_ref[:, cut], preferred_element_type=jnp.float32)
        out_here[:, cut] = (weight_here * produced[:half]).astype(jnp.bfloat16)
        out_there[:, cut] = (weight_there * produced[half:]).astype(jnp.bfloat16)


def expert_piece(here, there, experts, pieces, after=()):
    half = here.shape[0]
    hidden, width = pieces[2].shape
    out = pltpu.VMEM((half, width), jnp.bfloat16)
    vmem = whole(pltpu.VMEM)
    return pl.pallas_call(
        functools.partial(experts_kernel, experts, len(after)),
        out_shape=(out, out),
        in_specs=[vmem] * 5 + [whole(pl.ANY)] * len(after),
        out_specs=(vmem, vmem),
        scratch_shapes=[
            pltpu.VMEM((2 * half, width), jnp.bfloat16),
            pltpu.VMEM((2 * half, hidden), jnp.bfloat16),
        ],
        compiler_params=pltpu.CompilerParams(vmem_limit_bytes=64 * half * 1024 + 4 * MIB),
        cost_estimate=pl.CostEstimate(
            flops=12 * half * width * hidden, bytes_accessed=0, transcendentals=2 * half * hidden
        ),
        name="expert_piece",
    )(here, there, *pieces, *after)


def exchange(rows, node_mask, local_mask):
    nodes = lax.axis_size("node")
    locals_ = lax.axis_size("local")
    pairs = [
        (n * locals_ + k, (n ^ node_mask) * locals_ + (k ^ local_mask))
        for n in range(nodes)
        for k in range(locals_)
    ]
    return lax.ppermute(rows, ("node", "local"), pairs)


def masks():
    locals_, nodes = lax.axis_size("local"), lax.axis_size("node")
    near, far = list(range(locals_ // 2)), list(range(locals_ // 2, locals_))
    return near, far, list(range(nodes - 4, 0, -2)) + [nodes - 2]


def gather_plane(line, after=()):
    return pack([line] + [exchange(line, n, 0) for n in masks()[2]], after=after)


def f32(x):
    return x.astype(jnp.float32)


def block(x, size, i):
    return x[i * size : (i + 1) * size]


def core_sum(here, there):
    return f32(here) + f32(exchange(there, 1, 0))


def plane_sum(sums):
    plane = masks()[2]
    size = sums.shape[0] // (1 + len(plane))
    line, packed = sums[:size], sums.astype(jnp.bfloat16)
    for i, n in enumerate(plane):
        line = line + f32(exchange(block(packed, size, i + 1), n, 0))
    return line


def per_device(
    queries,
    key_cache,
    value_cache,
    fresh_token_keys,
    new_values,
    lengths,
    hidden_rows,
    norm_gain,
    expert_ids,
    route_scores,
    gate_weight,
    up_weight,
    down_weight,
):
    context = attend(queries, key_cache, value_cache, fresh_token_keys, new_values, lengths)
    experts = lax.axis_size("node") * lax.axis_size("local") // 2
    count = hidden_rows.shape[0]
    near, far, _ = masks()
    rows = prepare(hidden_rows, norm_gain, expert_ids, route_scores, experts)
    line = {k: exchange(rows, 0, k) for k in near[1:] + far}
    second = pack([line[k] for k in far], after=(in_hbm(context),))
    first = gather_plane(pack([rows] + [line[k] for k in near[1:]]), after=(second,))
    pieces = (gate_weight[0], up_weight[0], down_weight[0])
    first, first_other = expert_piece(first, exchange(first, 1, 0), experts, pieces)
    second = gather_plane(second, after=(first,))
    second, first_other = lax.optimization_barrier((second, first_other))
    second, second_other = expert_piece(second, exchange(second, 1, 0), experts, pieces)
    plane = masks()[2]
    sums = core_sum(second, second_other)
    size = sums.shape[0] // (1 + len(plane))
    packed, farther = sums.astype(jnp.bfloat16), sums[:size]
    arrived = [exchange(block(packed, size, i + 1), n, 0) for i, n in enumerate(plane)]
    arrived[0], nearer = lax.optimization_barrier((arrived[0], core_sum(first, first_other)))
    for piece in arrived:
        farther = farther + f32(piece)
    farther = farther.astype(jnp.bfloat16)
    nearer = plane_sum(nearer)
    total, packed = nearer[:count], nearer.astype(jnp.bfloat16)
    for i, k in enumerate(far):
        total = total + f32(exchange(block(farther, count, i), 0, k))
    for i, k in enumerate(near[1:]):
        total = total + f32(exchange(block(packed, count, i + 1), 0, k))
    total = total.astype(jnp.bfloat16)
    return (context, total)


def solution(mesh):
    placed = (
        P(("group", "node", "local"), None, None),
        P(("group", "node", "local"), None, None, None),
        P(("group", "node", "local"), None, None, None),
        P(("group", "node", "local"), None, None),
        P(("group", "node", "local"), None, None),
        P(("group", "node", "local")),
        P(("group", "node", "local"), None),
        P(),
        P(("group", "node", "local"), None),
        P(("group", "node", "local"), None),
        P(("node", "local"), None, None),
        P(("node", "local"), None, None),
        P(("node", "local"), None, None),
    )
    return jax.shard_map(
        per_device,
        mesh=mesh,
        in_specs=placed,
        out_specs=(P(("group", "node", "local"), None), P(("group", "node", "local"), None)),
        check_vma=False,
    )
```
